32 devices in a mesh: inv: 2 (over x), azim: 16 (over z, y, core).
Axes of the slice: x: 2, y: 2, z: 4, core: 2. Of those that a mesh axis runs over, the one named last changes fastest.
Arguments:
- forward_field: float32 [8, 64, 8, 1024], P('inv', 'azim'), parts along dimension 0, may hold values from -6 to 6
- conductivity: float32 [64, 16, 1024], P('azim', 'inv'), parts along dimension 1, may hold values from 0.1 to 10
- conductivity_mid: float32 [32, 8, 512], P('azim', 'inv'), parts along dimension 1, may hold values from 0.1 to 10
- conductivity_coarse: float32 [16, 4, 256], P('azim', 'inv'), parts along dimension 1, may hold values from 0.1 to 10
- receiver_cells: int32 [16, 8192], P('azim', 'inv'), parts along dimension 1, may hold values from 0 to 32767
- receiver_weights: float32 [8, 16, 4096], P('inv', 'azim'), parts along dimension 0, may hold values from -24 to 24
Outputs:
- adjoint_field: float32 [8, 64, 8, 1024], P('inv', 'azim'), parts along dimension 0
- gradient: float32 [64, 16, 1024], P('azim', 'inv'), parts along dimension 1
The draws below stay inside these ranges and needn't reach their ends.
There are 2 independent parts, one for each index of `inv`. The reference program is written for one: setup_inputs(seed, part) draws one part's arguments, and reference() takes and returns one part's arrays. A program takes and returns all parts, laid end to end along the dimension named above; each array names one. Nothing has to cross between parts.
Inputs may be any that keep to these rules, and one draw needn't show every extreme that they name: `receiver_cells`: each entry is a cell of the azimuth block of the device that holds it; several receivers may share a cell.
All inputs are finite; a program needn't handle non-finite values.
Results may differ from the reference program's by a relative error of at most 0.0001.
Values sent between devices are 32-bit elements; how exact they have to be, the bound alone decides.
A program may use at most 128 MiB of HBM per device.

```python
import math
import jax
import jax.numpy as jnp
from jax import lax

NR = 1024
AZ_DEV = 4
NZ = 8
RECV_DEV = 4096
SOURCES = 4
SWEEPS = 2
COARSE_SWEEPS = 4
CYCLES = 2
NA = 64
N_AZIM = 16


def set_ends(entries, key, smallest, high):
    shape = entries.shape
    index_at = [jax.random.randint(jax.random.fold_in(key, axis), (), 0, shape[axis]) for axis in range(len(shape))]
    entries = entries.at[tuple(index_at)].set(smallest)
    longest = shape.index(max(shape))
    index_at[longest] = (index_at[longest] + 1) % shape[longest]
    return entries.at[tuple(index_at)].set(high)


def level_of(own_key, shape, cuts, least, high):
    loudness = 1.0
    for axis_at, blocks in cuts:
        steps = jax.random.uniform(jax.random.fold_in(jax.random.fold_in(own_key, 6), axis_at), (blocks,), jnp.float32, least / len(cuts), high / len(cuts))
        loudness = loudness * jnp.repeat(jnp.exp(steps), shape[axis_at] // blocks).reshape((-1,) + (1,) * (len(shape) - 1 - axis_at))
    return loudness


def bell_draw(rng, dims, scale, most, split=(), held_as=jnp.bfloat16):
    entries = scale * jax.random.normal(rng, dims, jnp.float32)
    if split:
        entries = entries * level_of(rng, dims, split, -0.22, 0.18)
    return jnp.clip(entries, -most, most).astype(held_as)


def setup_inputs(seed: int = 0, part: int = 0) -> dict:
    splits = jax.random.split(jax.random.key(seed), 7)
    own_keys = jax.random.split(jax.random.fold_in(splits[6], part), 7)
    forward_field = bell_draw(own_keys[0], (SOURCES, NA, NZ, NR), 1.0, 6.0, ((1, 16),), jnp.float32)
    conductivity = jnp.clip(jnp.exp(math.log(10.0) - 4.6051702 * jax.random.uniform(own_keys[1], (NA, NZ, NR), jnp.float32) ** level_of(own_keys[1], (NA, NZ, NR), ((0, 16),), -0.2, 0.2)), 0.1, 10.0)
    conductivity_mid = jnp.clip(jnp.exp(math.log(10.0) - 4.6051702 * jax.random.uniform(own_keys[2], (NA // 2, NZ // 2, NR // 2), jnp.float32) ** level_of(own_keys[2], (NA // 2, NZ // 2, NR // 2), ((0, 16),), -0.2, 0.2)), 0.1, 10.0)
    conductivity_coarse = jnp.clip(jnp.exp(math.log(10.0) - 4.6051702 * jax.random.uniform(own_keys[3], (NA // 4, NZ // 4, NR // 4), jnp.float32) ** level_of(own_keys[3], (NA // 4, NZ // 4, NR // 4), ((0, 16),), -0.2, 0.2)), 0.1, 10.0)
    receiver_cells = set_ends(jax.random.randint(own_keys[4], (N_AZIM, RECV_DEV), 0, AZ_DEV * NZ * NR), jax.random.fold_in(own_keys[4], 1), 0, (AZ_DEV * NZ * NR) - 1).astype(jnp.int32)
    receiver_weights = bell_draw(own_keys[5], (SOURCES, N_AZIM, RECV_DEV), 4.0, 24.0, ((1, 16),), jnp.float32)
    return {"forward_field": forward_field, "conductivity": conductivity, "conductivity_mid": conductivity_mid, "conductivity_coarse": conductivity_coarse, "receiver_cells": receiver_cells, "receiver_weights": receiver_weights}


OMEGA = 0.7
BETA = 0.05


def geometry(spacing, radial, total_azim):
    inner = total_azim // 6
    theta = 2.0 * math.pi * spacing / total_azim
    index = jnp.arange(radial, dtype=jnp.float32)
    centre = inner + spacing * (index + 0.5)
    outer = inner + spacing * (index + 1.0)
    return centre, outer, theta


def wrapped(field, width, axis):
    length = field.shape[axis]
    return jnp.concatenate([lax.slice_in_dim(field, length - width, length, axis=axis), field,
                            lax.slice_in_dim(field, 0, width, axis=axis)], axis=axis)


def coefficients(sigma_ext, spacing, total_azim):
    centre, outer, theta = geometry(spacing, sigma_ext.shape[-1], total_azim)
    middle = sigma_ext[1:-1]
    radial_faces = outer[:-1] * theta * 0.5 * (middle[:, :, :-1] + middle[:, :, 1:])
    depth_faces = centre * theta * 0.5 * (middle[:, :-1, :] + middle[:, 1:, :])
    azim_faces = spacing * spacing / (centre * theta) * 0.5 * (sigma_ext[:-1] + sigma_ext[1:])
    radial_high = jnp.pad(radial_faces, ((0, 0), (0, 0), (0, 1)))
    radial_low = jnp.pad(radial_faces, ((0, 0), (0, 0), (1, 0)))
    depth_high = jnp.pad(depth_faces, ((0, 0), (0, 1), (0, 0)))
    depth_low = jnp.pad(depth_faces, ((0, 0), (1, 0), (0, 0)))
    diagonal = (radial_high + radial_low + depth_high + depth_low + azim_faces[:-1] + azim_faces[1:]
                + BETA * spacing * spacing * theta * centre * middle)
    return diagonal, azim_faces, radial_high, radial_low, depth_high, depth_low


def operate(padded, coeffs):
    diagonal, azim_faces, radial_high, radial_low, depth_high, depth_low = coeffs
    count = padded.shape[1] - 2
    offset = (diagonal.shape[0] - count) // 2
    faces = azim_faces[offset:offset + count + 1]
    middle = padded[:, 1:-1]
    edge_radial = jnp.zeros_like(middle[:, :, :, :1])
    edge_depth = jnp.zeros_like(middle[:, :, :1, :])
    outward = jnp.concatenate([middle[:, :, :, 1:], edge_radial], axis=3)
    inward = jnp.concatenate([edge_radial, middle[:, :, :, :-1]], axis=3)
    deeper = jnp.concatenate([middle[:, :, 1:, :], edge_depth], axis=2)
    higher = jnp.concatenate([edge_depth, middle[:, :, :-1, :]], axis=2)
    near = (faces[:-1] * padded[:, :-2] + faces[1:] * padded[:, 2:]
            + radial_high[offset:offset + count] * outward + radial_low[offset:offset + count] * inward
            + depth_high[offset:offset + count] * deeper + depth_low[offset:offset + count] * higher)
    own_diag = diagonal[offset:offset + count]
    return own_diag * middle - near, own_diag


def sweep(padded, right, coeffs):
    image, own_diag = operate(padded, coeffs)
    return padded[:, 1:-1] + OMEGA * ((right - image) / own_diag)


def restrict(field):
    shape = field.shape
    grouped = field.reshape(shape[0], shape[1] // 2, 2, shape[2] // 2, 2, shape[3] // 2, 2)
    return grouped.sum(axis=(2, 4, 6))


def prolong(field):
    return jnp.repeat(jnp.repeat(jnp.repeat(field, 2, axis=1), 2, axis=2), 2, axis=3)


def relax(field, right, coeffs, count):
    for turn in range(count):
        field = sweep(wrapped(field, 1, 1), right, coeffs)
    return field


def vcycle(field, right, levels):
    fine, middle_level, coarse = levels
    field = relax(field, right, fine, SWEEPS)
    image, unused = operate(wrapped(field, 1, 1), fine)
    right_mid = restrict(right - image)
    mid_field = relax(jnp.zeros_like(right_mid), right_mid, middle_level, SWEEPS)
    image_mid, unused = operate(wrapped(mid_field, 1, 1), middle_level)
    right_coarse = restrict(right_mid - image_mid)
    coarse_field = relax(jnp.zeros_like(right_coarse), right_coarse, coarse, COARSE_SWEEPS)
    mid_field = relax(mid_field + prolong(coarse_field), right_mid, middle_level, SWEEPS)
    return relax(field + prolong(mid_field), right, fine, SWEEPS)


def sensitivity(forward_pad, adjoint_pad, total_azim):
    centre, outer, theta = geometry(1, forward_pad.shape[-1], total_azim)
    forward_mid = forward_pad[:, 1:-1]
    adjoint_mid = adjoint_pad[:, 1:-1]
    azim = jnp.sum((forward_pad[:, 1:] - forward_pad[:, :-1]) * (adjoint_pad[:, 1:] - adjoint_pad[:, :-1]), axis=0)
    radial = jnp.sum((forward_mid[..., 1:] - forward_mid[..., :-1]) * (adjoint_mid[..., 1:] - adjoint_mid[..., :-1]), axis=0)
    radial = radial * (outer[:-1] * theta)
    depth = jnp.sum((forward_mid[:, :, 1:] - forward_mid[:, :, :-1]) * (adjoint_mid[:, :, 1:] - adjoint_mid[:, :, :-1]), axis=0)
    own = jnp.sum(forward_mid * adjoint_mid, axis=0)
    total = (0.5 / (centre * theta) * (azim[:-1] + azim[1:])
             + 0.5 * (jnp.pad(radial, ((0, 0), (0, 0), (1, 0))) + jnp.pad(radial, ((0, 0), (0, 0), (0, 1))))
             + 0.5 * centre * theta * (jnp.pad(depth, ((0, 0), (1, 0), (0, 0))) + jnp.pad(depth, ((0, 0), (0, 1), (0, 0))))
             + BETA * theta * centre * own)
    return -total


def reference(forward_field, conductivity, conductivity_mid, conductivity_coarse, receiver_cells, receiver_weights):
    block = AZ_DEV * NZ * NR
    owners = jnp.arange(N_AZIM, dtype=jnp.int32)[:, None] * block
    flat = (owners + receiver_cells.astype(jnp.int32)).reshape(-1)
    source = jnp.zeros((SOURCES, NA * NZ * NR), jnp.float32).at[:, flat].add(receiver_weights.reshape(SOURCES, -1))
    source = source.reshape(SOURCES, NA, NZ, NR)
    levels = (coefficients(wrapped(conductivity, 1, 0), 1, NA),
              coefficients(wrapped(conductivity_mid, 1, 0), 2, NA),
              coefficients(wrapped(conductivity_coarse, 1, 0), 4, NA))
    adjoint = jnp.zeros_like(source)
    for cycle in range(CYCLES):
        adjoint = vcycle(adjoint, source, levels)
    gradient = sensitivity(wrapped(forward_field, 1, 1), wrapped(adjoint, 1, 1), NA)
    return adjoint, gradient
```

```python
import functools
import math

import jax
import jax.numpy as jnp
from jax import lax
from jax.experimental import pallas as pl
from jax.experimental.pallas import tpu as pltpu
from jax.sharding import PartitionSpec as P

OMEGA = 0.7
BETA = 0.05
LANES = 128
F32 = jnp.float32
BF16 = jnp.bfloat16
MESH = pl.DeviceIdType.MESH
NT = (((1,), (1,)), ((), ()))


def pieces(x, count):
    out = []
    for _ in range(count):
        part = x.astype(BF16)
        out.append(part)
        x = x - part.astype(F32)
    return out


def scatter_kernel(cells_ref, weights_ref, out_ref):
    azim, sources, depth_j, depth, _ = out_ref.shape
    radial = depth_j * LANES
    half = depth_j // 2
    rows = azim * half * depth
    count = cells_ref.shape[1]
    cell = cells_ref[...]
    a = cell // (depth * radial)
    z = (cell // radial) % depth
    i = cell % radial
    lane = i // depth_j
    j = i % depth_j
    high = (a * half + j // 2) * depth + z
    low = (j % 2) * LANES + lane
    chunk = 1024
    totals = [jnp.zeros((rows, 2 * LANES), F32) for _ in range(sources)]
    for start in range(0, count, chunk):
        at = slice(start, start + chunk)
        hot_low = jnp.where(
            lax.broadcasted_iota(jnp.int32, (2 * LANES, chunk), 0) == low[:, at], 1.0, 0.0
        ).astype(BF16)
        hit = lax.broadcasted_iota(jnp.int32, (rows, chunk), 0) == high[:, at]
        for s in range(sources):
            for part in pieces(weights_ref[s, :, at], 2):
                left = jnp.where(hit, part.astype(F32), 0.0).astype(BF16)
                totals[s] = totals[s] + lax.dot_general(
                    left, hot_low, NT, preferred_element_type=F32
                )
    for s in range(sources):
        grid = totals[s].reshape(azim, half, depth, 2 * LANES)
        for jh in range(half):
            for jl in range(2):
                out_ref[:, s, 2 * jh + jl] = grid[:, jh, :, jl * LANES:(jl + 1) * LANES]


def roll(x, shift, axis):
    return pltpu.roll(x, shift % x.shape[axis], axis)


def outward(v):
    return jnp.concatenate([v[1:], roll(v[:1], -1, 2)], axis=0)


def inward(v):
    return jnp.concatenate([roll(v[-1:], 1, 2), v[:-1]], axis=0)


def sublane(shape):
    return lax.broadcasted_iota(jnp.int32, shape, len(shape) - 2)


def order(size):
    j = size // LANES
    row = lax.broadcasted_iota(jnp.int32, (size, size), 0)
    col = lax.broadcasted_iota(jnp.int32, (size, size), 1)
    return jnp.where(row == (col % LANES) * j + col // LANES, 1.0, 0.0).astype(BF16)


def reorder(rows, matrix, dims):
    total = None
    for part in pieces(rows, 3):
        term = lax.dot_general(part, matrix, dims, preferred_element_type=F32)
        total = term if total is None else total + term
    return total


def radius(j, inner, spacing):
    shape = (j, 8, LANES)
    index = lax.broadcasted_iota(jnp.int32, shape, 2) * j + lax.broadcasted_iota(jnp.int32, shape, 0)
    index = index.astype(F32)
    return inner + spacing * (index + 0.5), inner + spacing * (index + 1.0), index


def arrange(raw_ref, out_ref, matrix, first, last):
    depth, size = raw_ref.shape[1:]
    cells = last - first
    if depth == 8:
        full = raw_ref[first:last]
    else:
        each = 8 // depth
        at = sublane((cells, 8, size)) // each
        full = jnp.broadcast_to(raw_ref[first:last, 0:1, :], (cells, 8, size))
        for z in range(1, depth):
            full = jnp.where(at == z, jnp.broadcast_to(raw_ref[first:last, z:z + 1, :], (cells, 8, size)), full)
    out = reorder(full.reshape(cells * 8, size), matrix, (((1,), (0,)), ((), ())))
    for j in range(size // LANES):
        out_ref[first:last, j] = out[:, j * LANES:(j + 1) * LANES].reshape(cells, 8, LANES)


class Level:
    def __init__(self, refs, shift, spacing, inner, theta):
        self.sigma, self.face, self.radial, self.deep, self.diag, self.scale = refs
        self.shift = shift
        self.spacing = spacing
        self.inner = inner
        self.theta = theta
        self.count, self.j = self.sigma.shape[:2]

    def coefficients(self):
        h, theta, k, j = self.spacing, self.theta, self.shift, self.j
        centre, outer, index = radius(j, self.inner, h)
        to_radial = jnp.where(index < j * LANES - 1, outer * (theta * 0.5), 0.0)
        to_deep = jnp.where(sublane(centre.shape) < 8 - k, centre * (theta * 0.5), 0.0)
        to_face = (0.5 * h * h / theta) / centre
        to_own = (BETA * h * h * theta) * centre

        def faces(c, carry):
            self.face[c] = to_face * (self.sigma[c - 1] + self.sigma[c])
            return carry

        lax.fori_loop(1, self.count, faces, 0)

        def cell(c, carry):
            own = self.sigma[c]
            radial = to_radial * (own + outward(own))
            deep = to_deep * (own + roll(own, -k, 1))
            diag = (radial + inward(radial) + deep + roll(deep, k, 1)
                    + self.face[c] + self.face[c + 1] + to_own * own)
            self.radial[c] = radial
            self.deep[c] = deep
            self.diag[c] = diag
            self.scale[c] = OMEGA / diag
            return carry

        lax.fori_loop(1, self.count - 1, cell, 0)

    def near(self, field, c, g):
        v = field[c, g]
        radial, deep, k = self.radial[c], self.deep[c], self.shift
        return v, (self.face[c] * field[c - 1, g] + self.face[c + 1] * field[c + 1, g]
                   + radial * outward(v) + inward(radial * v)
                   + deep * roll(v, -k, 1) + roll(deep * v, k, 1))

    def first(self, right, out, lo, hi):
        def body(c, carry):
            scale = self.scale[c]
            for g in range(right.shape[1]):
                out[c, g] = scale * right[c, g]
            return carry

        lax.fori_loop(lo, hi, body, 0)

    def sweep(self, field, out, right, lo, hi):
        def body(c, carry):
            for g in range(right.shape[1]):
                v, near = self.near(field, c, g)
                out[c, g] = (1.0 - OMEGA) * v + self.scale[c] * (right[c, g] + near)
            return carry

        lax.fori_loop(lo, hi, body, 0)

    def residual(self, field, right, c, g):
        v, near = self.near(field, c, g)
        return right[c, g] - self.diag[c] * v + near


def pair_sum(x, k):
    lower = (sublane(x.shape) // k) % 2 == 0
    return x + jnp.where(lower, roll(x, -k, x.ndim - 2), roll(x, k, x.ndim - 2))


def halve(x):
    return x.reshape((x.shape[0] // 2, 2) + x.shape[1:]).sum(axis=1)


def twice(x):
    shape = x.shape
    wide = jnp.broadcast_to(x[:, None], (shape[0], 2) + shape[1:])
    return wide.reshape((2 * shape[0],) + shape[1:])


def spread(x, k, which):
    odd = (sublane(x.shape) // k) % 2 == 1
    if which == 0:
        return twice(jnp.where(odd, roll(x, k, 1), x))
    return twice(jnp.where(odd, x, roll(x, -k, 1)))


def restrict(level, field, right, out, first, target, cells, k):
    for m in range(cells):
        for q in range(right.shape[1] // 2):
            sums = []
            for g in (2 * q, 2 * q + 1):
                both = (level.residual(field, right, first + 2 * m, g)
                        + level.residual(field, right, first + 2 * m + 1, g))
                sums.append(pair_sum(halve(both), k))
            odd = (sublane(sums[0].shape) // k) % 2 == 1
            out[target + m, q] = jnp.where(odd, sums[1], sums[0])


def prolong(field, coarse, out, lo, hi, offset, k):
    def body(c, carry):
        for q in range(coarse.shape[1]):
            x = coarse[c // 2 + offset, q]
            for which in range(2):
                g = 2 * q + which
                out[c, g] = field[c, g] + spread(x, k, which)
        return carry

    lax.fori_loop(lo, hi, body, 0)


def kernel(ring, inner, theta, forward_ref, sig0_ref, sig1_ref, sig2_ref, b_ref, adj_ref, grad_ref,
           raw0, raw1, raw2, uedge, *rest):
    rest = list(rest)
    refs = [[rest.pop(0) for _ in range(6)] for _ in range(3)]
    B, VA, VB, VC, VD = [rest.pop(0) for _ in range(5)]
    MA, MD, CA, CB = [rest.pop(0) for _ in range(4)]
    cyc = [[rest.pop(0) for _ in range(4)] for _ in range(2)]
    wide, send_sems, recv_sems = rest
    sources = forward_ref.shape[0]
    size = forward_ref.shape[-1]
    me = lax.axis_index("azim")
    inv = lax.axis_index("inv")
    used = []

    def device(offset):
        return (inv, lax.rem(me + offset + ring, ring))

    def send(src, dst, offset):
        n = len(used)
        copy = pltpu.make_async_remote_copy(
            src_ref=src, dst_ref=dst, send_sem=send_sems.at[n], recv_sem=recv_sems.at[n],
            device_id=device(offset), device_id_type=MESH)
        copy.start()
        used.append(copy)
        return copy

    def arrived(copies):
        for copy in copies:
            copy.wait_recv()

    barrier = pltpu.get_barrier_semaphore()
    offsets = [s * k for k in range(1, 6) for s in (1, -1)]
    for offset in offsets:
        pl.semaphore_signal(barrier, inc=1, device_id=device(offset), device_id_type=MESH)
    pl.semaphore_wait(barrier, len(offsets))

    got_sigma = [
        send(sig0_ref, raw0.at[0:4], 1), send(sig0_ref, raw0.at[8:12], -1),
        send(sig1_ref, raw1.at[2:4], 1), send(sig1_ref, raw1.at[6:8], -1),
        send(sig1_ref, raw1.at[0:2], 2), send(sig1_ref, raw1.at[8:10], -2),
    ]
    for k in range(1, 6):
        got_sigma.append(send(sig2_ref, raw2.at[5 - k:6 - k], k))
        got_sigma.append(send(sig2_ref, raw2.at[5 + k:6 + k], -k))
    got_b = [send(b_ref.at[2:4], B.at[2:4], 1), send(b_ref.at[0:2], B.at[8:10], -1)]
    got_b_far = [send(b_ref.at[1:2], B.at[1:2], 1), send(b_ref.at[2:3], B.at[10:11], -1)]
    got_u = [send(forward_ref.at[:, 3:4], uedge.at[0], 1), send(forward_ref.at[:, 0:1], uedge.at[1], -1)]

    raw0[4:8] = sig0_ref[...]
    raw1[4:6] = sig1_ref[...]
    raw2[5:6] = sig2_ref[...]
    B[4:8] = b_ref[...]
    wide[...] = order(size)
    mid_order = order(size // 2)
    coarse_order = order(size // 4)

    fine = Level(refs[0], 1, 1, inner, theta)
    mid = Level(refs[1], 2, 2, inner, 2 * theta)
    coarse = Level(refs[2], 4, 4, inner, 4 * theta)
    arrived(got_sigma)
    arrange(raw0, fine.sigma, wide[...], 0, 12)
    fine.coefficients()
    arrange(raw1, mid.sigma, mid_order, 0, 10)
    mid.coefficients()
    arrange(raw2, coarse.sigma, coarse_order, 0, 11)
    coarse.coefficients()

    def correction(field, buffers):
        B1, MB, B2, ME = buffers
        restrict(fine, field, B, B1, 4, 4, 2, 1)
        got = [send(B1.at[4:6], B1.at[2:4], 1), send(B1.at[4:6], B1.at[6:8], -1)]
        if field is VB:
            got_far = [send(VB.at[4:7], VB.at[0:3], 1), send(VB.at[5:8], VB.at[9:12], -1)]
        else:
            got_far = [send(VD.at[5:7], VD.at[1:3], 1), send(VD.at[5:7], VD.at[9:11], -1)]
        arrived(got)
        mid.first(B1, MA, 2, 8)
        mid.sweep(MA, MB, B1, 3, 7)
        restrict(mid, MB, B1, B2, 4, 5, 1, 2)
        got = []
        for k in range(1, 5):
            got.append(send(B2.at[5:6], B2.at[5 - k:6 - k], k))
            got.append(send(B2.at[5:6], B2.at[5 + k:6 + k], -k))
        got_mid = [send(MB.at[4:5], MB.at[2:3], 1), send(MB.at[5:6], MB.at[7:8], -1)]
        arrived(got)
        coarse.first(B2, CA, 1, 10)
        coarse.sweep(CA, CB, B2, 2, 9)
        coarse.sweep(CB, CA, B2, 3, 8)
        coarse.sweep(CA, CB, B2, 4, 7)
        arrived(got_mid)
        prolong(MB, CB, MA, 2, 8, 3, 2)
        mid.sweep(MA, MD, B1, 3, 7)
        mid.sweep(MD, ME, B1, 4, 6)
        got = [send(ME.at[4:6], ME.at[2:4], 1), send(ME.at[4:6], ME.at[6:8], -1)]
        arrived(got_far)
        arrived(got)
        return ME

    arrived(got_b)
    fine.first(B, VA, 2, 10)
    fine.sweep(VA, VB, B, 3, 9)
    fix = correction(VB, cyc[0])
    arrived(got_b_far)
    prolong(VB, fix, VA, 0, 12, 2, 1)
    fine.sweep(VA, VC, B, 1, 11)
    fine.sweep(VC, VA, B, 2, 10)
    fine.sweep(VA, VC, B, 3, 9)
    fine.sweep(VC, VD, B, 4, 8)
    arrived([send(VD.at[7:8], VD.at[3:4], 1), send(VD.at[4:5], VD.at[8:9], -1)])
    fix = correction(VD, cyc[1])
    prolong(VD, fix, VA, 1, 11, 2, 1)
    fine.sweep(VA, VC, B, 2, 10)
    fine.sweep(VC, VA, B, 3, 9)

    def natural(lo, hi):
        cells = hi - lo
        rows = jnp.concatenate(
            [VA[lo:hi, :, j].reshape(cells * sources * 8, LANES) for j in range(size // LANES)], axis=1)
        return reorder(rows, wide[...], NT).reshape(cells, sources, 8, size)

    w = natural(3, 9)
    lane = lax.broadcasted_iota(jnp.int32, (8, size), 1)
    index = lane.astype(F32)
    centre = inner + (index + 0.5)
    outer = inner + (index + 1.0)
    to_radial = jnp.where(lane < size - 1, outer * (0.5 * theta), 0.0)
    to_deep = jnp.where(sublane((8, size)) < 7, centre * (0.5 * theta), 0.0)
    to_azim = (0.5 / theta) / centre
    to_own = (BETA * theta) * centre
    arrived(got_u)

    def forward_at(c, s):
        if c < 0:
            return uedge[0, s, 0]
        if c > 3:
            return uedge[1, s, 0]
        return forward_ref[s, c]

    face = None
    for c in range(-1, 4):
        total = None
        for s in range(sources):
            term = (forward_at(c + 1, s) - forward_at(c, s)) * (w[c + 2, s] - w[c + 1, s])
            total = term if total is None else total + term
        before, face = face, total
        if c < 0:
            continue
        radial = deep = own = None
        for s in range(sources):
            u, x = forward_at(c, s), w[c + 1, s]
            adj_ref[s, c] = x
            terms = ((roll(u, -1, 1) - u) * (roll(x, -1, 1) - x),
                     (roll(u, -1, 0) - u) * (roll(x, -1, 0) - x), u * x)
            if s == 0:
                radial, deep, own = terms
            else:
                radial, deep, own = radial + terms[0], deep + terms[1], own + terms[2]
        radial = radial * to_radial
        deep = deep * to_deep
        grad_ref[c] = -(to_azim * (before + face) + radial + roll(radial, 1, 1)
                        + deep + roll(deep, 1, 0) + to_own * own)

    for copy in used:
        copy.wait_send()


def local(forward_field, conductivity, conductivity_mid, conductivity_coarse, receiver_cells, receiver_weights):
    sources, azim, depth, size = forward_field.shape
    ring = lax.axis_size("azim")
    total_azim = azim * ring
    inner = total_azim // 6
    theta = 2.0 * math.pi / total_azim
    j = size // LANES
    vmem = pl.BlockSpec(memory_space=pltpu.VMEM)
    source = pl.pallas_call(
        scatter_kernel,
        out_shape=jax.ShapeDtypeStruct((azim, sources, j, depth, LANES), F32),
        in_specs=[vmem] * 2,
        out_specs=vmem,
        compiler_params=pltpu.CompilerParams(vmem_limit_bytes=48 * 1024 * 1024),
    )(receiver_cells, receiver_weights)

    def field(cells, groups, level_j):
        return pltpu.VMEM((cells, groups, level_j, 8, LANES), F32)

    def level(cells, level_j):
        return [pltpu.VMEM((cells, level_j, 8, LANES), F32)] * 6

    one_cycle = [field(10, 2, j // 2), field(10, 2, j // 2), field(11, 1, j // 4), field(10, 2, j // 2)]
    scratch = [
        pltpu.VMEM((12, depth, size), F32),
        pltpu.VMEM((10, depth // 2, size // 2), F32),
        pltpu.VMEM((11, depth // 4, size // 4), F32),
        pltpu.VMEM((2, sources, 1, depth, size), F32),
        *level(12, j), *level(10, j // 2), *level(11, j // 4),
        *[field(12, sources, j)] * 5,
        *[field(10, 2, j // 2)] * 2,
        *[field(11, 1, j // 4)] * 2,
        *one_cycle, *one_cycle,
        pltpu.VMEM((size, size), BF16),
        pltpu.SemaphoreType.DMA((64,)),
        pltpu.SemaphoreType.DMA((64,)),
    ]
    return pl.pallas_call(
        functools.partial(kernel, ring, inner, theta),
        out_shape=(
            jax.ShapeDtypeStruct((sources, azim, depth, size), F32),
            jax.ShapeDtypeStruct((azim, depth, size), F32),
        ),
        in_specs=[vmem] * 5,
        out_specs=(vmem, vmem),
        scratch_shapes=scratch,
        compiler_params=pltpu.CompilerParams(
            collective_id=0, has_side_effects=True, vmem_limit_bytes=48 * 1024 * 1024),
    )(forward_field, conductivity, conductivity_mid, conductivity_coarse, source)


def solution(mesh):
    placed = (
        P("inv", "azim", None, None),
        P("azim", "inv", None),
        P("azim", "inv", None),
        P("azim", "inv", None),
        P("azim", "inv"),
        P("inv", "azim", None),
    )
    return jax.shard_map(
        local,
        mesh=mesh,
        in_specs=placed,
        out_specs=(P("inv", "azim", None, None), P("azim", "inv", None)),
        check_vma=False,
    )
```

```python
import functools
import math

import jax
import jax.numpy as jnp
from jax import lax
from jax.experimental import pallas as pl
from jax.experimental.pallas import tpu as pltpu
from jax.sharding import PartitionSpec as P

OMEGA = 0.7
BETA = 0.05
LANES = 128
F32 = jnp.float32
BF16 = jnp.bfloat16
MESH = pl.DeviceIdType.MESH
NT = (((1,), (1,)), ((), ()))


def pieces(x, count):
    out = []
    for _ in range(count):
        part = x.astype(BF16)
        out.append(part)
        x = x - part.astype(F32)
    return out


def log2(n):
    assert n & (n - 1) == 0
    return n.bit_length() - 1


def scatter(cells_ref, weights_ref, out_ref):
    azim, sources, depth_j, depth, _ = out_ref.shape
    radial = depth_j * LANES
    half = depth_j // 2
    rows = azim * half * depth
    count = cells_ref.shape[1]
    cell = cells_ref[...]
    a = cell >> log2(depth * radial)
    z = (cell >> log2(radial)) & (depth - 1)
    i = cell & (radial - 1)
    lane = i >> log2(depth_j)
    j = i & (depth_j - 1)
    high = (a * half + (j >> 1)) * depth + z
    low = (j & 1) * LANES + lane
    chunk = 1024
    total = jnp.zeros((2 * sources * rows, 2 * LANES), F32)
    for start in range(0, count, chunk):
        at = slice(start, start + chunk)
        hot_low = jnp.where(
            lax.broadcasted_iota(jnp.int32, (2 * LANES, chunk), 0) == low[:, at], 1.0, 0.0
        ).astype(BF16)
        hit = lax.broadcasted_iota(jnp.int32, (rows, chunk), 0) == high[:, at]
        left = []
        for s in range(sources):
            for part in pieces(weights_ref[s, :, at], 2):
                left.append(jnp.where(hit, part.astype(F32), 0.0).astype(BF16))
        total = total + lax.dot_general(
            jnp.concatenate(left, axis=0), hot_low, NT, preferred_element_type=F32
        )
    for s in range(sources):
        first = 2 * s * rows
        both = total[first:first + rows] + total[first + rows:first + 2 * rows]
        grid = both.reshape(azim, half, depth, 2 * LANES)
        for jh in range(half):
            for jl in range(2):
                out_ref[:, s, 2 * jh + jl] = grid[:, jh, :, jl * LANES:(jl + 1) * LANES]


def roll(x, shift, axis):
    return pltpu.roll(x, shift % x.shape[axis], axis)


def outward(v):
    return jnp.concatenate([v[1:], roll(v[:1], -1, 2)], axis=0)


def inward(v):
    return jnp.concatenate([roll(v[-1:], 1, 2), v[:-1]], axis=0)


def sublane(shape):
    return lax.broadcasted_iota(jnp.int32, shape, len(shape) - 2)


def order(size):
    j = size // LANES
    row = lax.broadcasted_iota(jnp.int32, (size, size), 0)
    col = lax.broadcasted_iota(jnp.int32, (8, size), 1)
    want = ((col & (LANES - 1)) * j + (col >> log2(LANES)))[0:1]
    return jnp.where(row == want, 1.0, 0.0).astype(BF16)


def reorder(rows, matrix, dims):
    count = rows.shape[0]
    stacked = jnp.concatenate(pieces(rows, 3), axis=0)
    out = lax.dot_general(stacked, matrix, dims, preferred_element_type=F32)
    return out[:count] + out[count:2 * count] + out[2 * count:]


def radius(j, inner, spacing):
    shape = (j, 8, LANES)
    index = lax.broadcasted_iota(jnp.int32, shape, 2) * j + lax.broadcasted_iota(jnp.int32, shape, 0)
    index = index.astype(F32)
    return inner + spacing * (index + 0.5), inner + spacing * (index + 1.0), index


def arrange(raw_ref, out_ref, matrix, first, last):
    depth, size = raw_ref.shape[1:]
    cells = last - first
    if depth == 8:
        full = raw_ref[first:last]
    else:
        each = 8 // depth
        at = sublane((cells, 8, size)) // each
        full = jnp.broadcast_to(raw_ref[first:last, 0:1, :], (cells, 8, size))
        for z in range(1, depth):
            full = jnp.where(at == z, jnp.broadcast_to(raw_ref[first:last, z:z + 1, :], (cells, 8, size)), full)
    out = reorder(full.reshape(cells * 8, size), matrix, (((1,), (0,)), ((), ())))
    for j in range(size // LANES):
        out_ref[first:last, j] = out[:, j * LANES:(j + 1) * LANES].reshape(cells, 8, LANES)


class Level:
    def __init__(self, refs, shift, spacing, inner, theta):
        self.sigma, self.face, self.radial, self.deep, self.diag, self.scale = refs
        self.shift = shift
        self.spacing = spacing
        self.inner = inner
        self.theta = theta
        self.count, self.j = self.sigma.shape[:2]

    def coefficients(self):
        h, theta, k, j = self.spacing, self.theta, self.shift, self.j
        centre, outer, index = radius(j, self.inner, h)
        to_radial = jnp.where(index < j * LANES - 1, outer * (theta * 0.5), 0.0)
        to_deep = jnp.where(sublane(centre.shape) < 8 - k, centre * (theta * 0.5), 0.0)
        to_face = (0.5 * h * h / theta) / centre
        to_own = (BETA * h * h * theta) * centre

        def faces(c, carry):
            self.face[c] = to_face * (self.sigma[c - 1] + self.sigma[c])
            return carry

        lax.fori_loop(1, self.count, faces, 0)

        def cell(c, carry):
            own = self.sigma[c]
            radial = to_radial * (own + outward(own))
            deep = to_deep * (own + roll(own, -k, 1))
            diag = (radial + inward(radial) + deep + roll(deep, k, 1)
                    + self.face[c] + self.face[c + 1] + to_own * own)
            self.radial[c] = radial
            self.deep[c] = deep
            self.diag[c] = diag
            self.scale[c] = OMEGA / diag
            return carry

        lax.fori_loop(1, self.count - 1, cell, 0)

    def near(self, field, c, g):
        v = field[c, g]
        radial, deep, k = self.radial[c], self.deep[c], self.shift
        return v, (self.face[c] * field[c - 1, g] + self.face[c + 1] * field[c + 1, g]
                   + radial * outward(v) + inward(radial * v)
                   + deep * roll(v, -k, 1) + roll(deep * v, k, 1))

    def first(self, right, out, lo, hi):
        def body(c, carry):
            scale = self.scale[c]
            for g in range(right.shape[1]):
                out[c, g] = scale * right[c, g]
            return carry

        lax.fori_loop(lo, hi, body, 0)

    def sweep(self, field, out, right, lo, hi):
        def body(c, carry):
            for g in range(right.shape[1]):
                v, near = self.near(field, c, g)
                out[c, g] = (1.0 - OMEGA) * v + self.scale[c] * (right[c, g] + near)
            return carry

        lax.fori_loop(lo, hi, body, 0)

    def residual(self, field, right, c, g):
        v, near = self.near(field, c, g)
        return right[c, g] - self.diag[c] * v + near


def pair_sum(x, k):
    lower = (sublane(x.shape) // k) % 2 == 0
    return x + jnp.where(lower, roll(x, -k, x.ndim - 2), roll(x, k, x.ndim - 2))


def halve(x):
    return x.reshape((x.shape[0] // 2, 2) + x.shape[1:]).sum(axis=1)


def twice(x):
    shape = x.shape
    wide = jnp.broadcast_to(x[:, None], (shape[0], 2) + shape[1:])
    return wide.reshape((2 * shape[0],) + shape[1:])


def spread(x, k, which):
    odd = (sublane(x.shape) // k) % 2 == 1
    if which == 0:
        return twice(jnp.where(odd, roll(x, k, 1), x))
    return twice(jnp.where(odd, x, roll(x, -k, 1)))


def restrict(level, field, right, out, first, target, cells, k):
    for m in range(cells):
        for q in range(right.shape[1] // 2):
            sums = []
            for g in (2 * q, 2 * q + 1):
                both = (level.residual(field, right, first + 2 * m, g)
                        + level.residual(field, right, first + 2 * m + 1, g))
                sums.append(pair_sum(halve(both), k))
            odd = (sublane(sums[0].shape) // k) % 2 == 1
            out[target + m, q] = jnp.where(odd, sums[1], sums[0])


def prolong(field, coarse, out, lo, hi, offset, k):
    def body(c, carry):
        for q in range(coarse.shape[1]):
            x = coarse[c // 2 + offset, q]
            for which in range(2):
                g = 2 * q + which
                out[c, g] = field[c, g] + spread(x, k, which)
        return carry

    lax.fori_loop(lo, hi, body, 0)


def kernel(ring, inner, theta, forward_ref, sig0_ref, sig1_ref, sig2_ref, cells_ref, weights_ref, adj_ref, grad_ref,
           raw0, raw1, raw2, uedge, *rest):
    rest = list(rest)
    refs = [[rest.pop(0) for _ in range(6)] for _ in range(3)]
    B, VA, VB, VC, VD = [rest.pop(0) for _ in range(5)]
    MA, MD, CA, CB = [rest.pop(0) for _ in range(4)]
    cyc = [[rest.pop(0) for _ in range(4)] for _ in range(2)]
    wide, send_sems, recv_sems = rest
    sources = forward_ref.shape[0]
    size = forward_ref.shape[-1]
    me = lax.axis_index("azim")
    inv = lax.axis_index("inv")
    used = []

    def device(offset):
        return (inv, lax.rem(me + offset + ring, ring))

    def send(src, dst, offset):
        n = len(used)
        copy = pltpu.make_async_remote_copy(
            src_ref=src, dst_ref=dst, send_sem=send_sems.at[n], recv_sem=recv_sems.at[n],
            device_id=device(offset), device_id_type=MESH)
        copy.start()
        used.append(copy)
        return copy

    def arrived(copies):
        for copy in copies:
            copy.wait_recv()

    barrier = pltpu.get_barrier_semaphore()
    offsets = [s * k for k in range(1, 6) for s in (1, -1)]
    for offset in offsets:
        pl.semaphore_signal(barrier, inc=1, device_id=device(offset), device_id_type=MESH)
    pl.semaphore_wait(barrier, len(offsets))

    got_sigma = [
        send(sig0_ref, raw0.at[0:4], 1), send(sig0_ref, raw0.at[8:12], -1),
        send(sig1_ref, raw1.at[2:4], 1), send(sig1_ref, raw1.at[6:8], -1),
        send(sig1_ref, raw1.at[0:2], 2), send(sig1_ref, raw1.at[8:10], -2),
    ]
    for k in range(1, 6):
        got_sigma.append(send(sig2_ref, raw2.at[5 - k:6 - k], k))
        got_sigma.append(send(sig2_ref, raw2.at[5 + k:6 + k], -k))
    got_u = [send(forward_ref.at[:, 3:4], uedge.at[0], 1), send(forward_ref.at[:, 0:1], uedge.at[1], -1)]

    raw0[4:8] = sig0_ref[...]
    raw1[4:6] = sig1_ref[...]
    raw2[5:6] = sig2_ref[...]
    scatter(cells_ref, weights_ref, B.at[4:8])
    got_b = [send(B.at[6:8], B.at[2:4], 1), send(B.at[4:6], B.at[8:10], -1)]
    wide[...] = order(size)
    mid_order = order(size // 2)
    coarse_order = order(size // 4)

    fine = Level(refs[0], 1, 1, inner, theta)
    mid = Level(refs[1], 2, 2, inner, 2 * theta)
    coarse = Level(refs[2], 4, 4, inner, 4 * theta)
    arrived(got_sigma)
    arrange(raw0, fine.sigma, wide[...], 0, 12)
    fine.coefficients()
    arrange(raw1, mid.sigma, mid_order, 0, 10)
    mid.coefficients()
    arrange(raw2, coarse.sigma, coarse_order, 0, 11)
    coarse.coefficients()

    def correction(field, buffers):
        B1, MB, B2, ME = buffers
        restrict(fine, field, B, B1, 4, 4, 2, 1)
        got = [send(B1.at[4:6], B1.at[2:4], 1), send(B1.at[4:6], B1.at[6:8], -1)]
        if field is VB:
            got_far = [send(VB.at[4:7], VB.at[0:3], 1), send(VB.at[5:8], VB.at[9:12], -1)]
        else:
            got_far = [send(VD.at[5:7], VD.at[1:3], 1), send(VD.at[5:7], VD.at[9:11], -1)]
        arrived(got)
        mid.first(B1, MA, 2, 8)
        mid.sweep(MA, MB, B1, 3, 7)
        restrict(mid, MB, B1, B2, 4, 5, 1, 2)
        got = []
        for k in range(1, 5):
            got.append(send(B2.at[5:6], B2.at[5 - k:6 - k], k))
            got.append(send(B2.at[5:6], B2.at[5 + k:6 + k], -k))
        got_mid = [send(MB.at[4:5], MB.at[2:3], 1), send(MB.at[5:6], MB.at[7:8], -1)]
        arrived(got)
        coarse.first(B2, CA, 1, 10)
        coarse.sweep(CA, CB, B2, 2, 9)
        coarse.sweep(CB, CA, B2, 3, 8)
        coarse.sweep(CA, CB, B2, 4, 7)
        arrived(got_mid)
        prolong(MB, CB, MA, 2, 8, 3, 2)
        mid.sweep(MA, MD, B1, 3, 7)
        mid.sweep(MD, ME, B1, 4, 6)
        got = [send(ME.at[4:6], ME.at[2:4], 1), send(ME.at[4:6], ME.at[6:8], -1)]
        arrived(got_far)
        arrived(got)
        return ME

    arrived(got_b)
    got_b_far = [send(B.at[5:6], B.at[1:2], 1), send(B.at[6:7], B.at[10:11], -1)]
    fine.first(B, VA, 2, 10)
    fine.sweep(VA, VB, B, 3, 9)
    fix = correction(VB, cyc[0])
    arrived(got_b_far)
    prolong(VB, fix, VA, 0, 12, 2, 1)
    fine.sweep(VA, VC, B, 1, 11)
    fine.sweep(VC, VA, B, 2, 10)
    fine.sweep(VA, VC, B, 3, 9)
    fine.sweep(VC, VD, B, 4, 8)
    arrived([send(VD.at[7:8], VD.at[3:4], 1), send(VD.at[4:5], VD.at[8:9], -1)])
    fix = correction(VD, cyc[1])
    prolong(VD, fix, VA, 1, 11, 2, 1)
    fine.sweep(VA, VC, B, 2, 10)
    fine.sweep(VC, VA, B, 3, 9)

    def natural(lo, hi):
        cells = hi - lo
        rows = jnp.concatenate(
            [VA[lo:hi, :, j].reshape(cells * sources * 8, LANES) for j in range(size // LANES)], axis=1)
        return reorder(rows, wide[...], NT).reshape(cells, sources, 8, size)

    w = natural(3, 9)
    lane = lax.broadcasted_iota(jnp.int32, (8, size), 1)
    index = lane.astype(F32)
    centre = inner + (index + 0.5)
    outer = inner + (index + 1.0)
    to_radial = jnp.where(lane < size - 1, outer * (0.5 * theta), 0.0)
    to_deep = jnp.where(sublane((8, size)) < 7, centre * (0.5 * theta), 0.0)
    to_azim = (0.5 / theta) / centre
    to_own = (BETA * theta) * centre
    arrived(got_u)

    def forward_at(c, s):
        if c < 0:
            return uedge[0, s, 0]
        if c > 3:
            return uedge[1, s, 0]
        return forward_ref[s, c]

    face = None
    for c in range(-1, 4):
        total = None
        for s in range(sources):
            term = (forward_at(c + 1, s) - forward_at(c, s)) * (w[c + 2, s] - w[c + 1, s])
            total = term if total is None else total + term
        before, face = face, total
        if c < 0:
            continue
        radial = deep = own = None
        for s in range(sources):
            u, x = forward_at(c, s), w[c + 1, s]
            adj_ref[s, c] = x
            terms = ((roll(u, -1, 1) - u) * (roll(x, -1, 1) - x),
                     (roll(u, -1, 0) - u) * (roll(x, -1, 0) - x), u * x)
            if s == 0:
                radial, deep, own = terms
            else:
                radial, deep, own = radial + terms[0], deep + terms[1], own + terms[2]
        radial = radial * to_radial
        deep = deep * to_deep
        grad_ref[c] = -(to_azim * (before + face) + radial + roll(radial, 1, 1)
                        + deep + roll(deep, 1, 0) + to_own * own)

    for copy in used:
        copy.wait_send()


def local(forward_field, conductivity, conductivity_mid, conductivity_coarse, receiver_cells, receiver_weights):
    sources, azim, depth, size = forward_field.shape
    ring = lax.axis_size("azim")
    total_azim = azim * ring
    inner = total_azim // 6
    theta = 2.0 * math.pi / total_azim
    j = size // LANES
    vmem = pl.BlockSpec(memory_space=pltpu.VMEM)
    def field(cells, groups, level_j):
        return pltpu.VMEM((cells, groups, level_j, 8, LANES), F32)

    def level(cells, level_j):
        return [pltpu.VMEM((cells, level_j, 8, LANES), F32)] * 6

    one_cycle = [field(10, 2, j // 2), field(10, 2, j // 2), field(11, 1, j // 4), field(10, 2, j // 2)]
    scratch = [
        pltpu.VMEM((12, depth, size), F32),
        pltpu.VMEM((10, depth // 2, size // 2), F32),
        pltpu.VMEM((11, depth // 4, size // 4), F32),
        pltpu.VMEM((2, sources, 1, depth, size), F32),
        *level(12, j), *level(10, j // 2), *level(11, j // 4),
        *[field(12, sources, j)] * 5,
        *[field(10, 2, j // 2)] * 2,
        *[field(11, 1, j // 4)] * 2,
        *one_cycle, *one_cycle,
        pltpu.VMEM((size, size), BF16),
        pltpu.SemaphoreType.DMA((64,)),
        pltpu.SemaphoreType.DMA((64,)),
    ]
    return pl.pallas_call(
        functools.partial(kernel, ring, inner, theta),
        out_shape=(
            jax.ShapeDtypeStruct((sources, azim, depth, size), F32),
            jax.ShapeDtypeStruct((azim, depth, size), F32),
        ),
        in_specs=[vmem] * 6,
        out_specs=(vmem, vmem),
        scratch_shapes=scratch,
        compiler_params=pltpu.CompilerParams(
            collective_id=0, has_side_effects=True, vmem_limit_bytes=48 * 1024 * 1024),
    )(forward_field, conductivity, conductivity_mid, conductivity_coarse, receiver_cells, receiver_weights)


def solution(mesh):
    placed = (
        P("inv", "azim", None, None),
        P("azim", "inv", None),
        P("azim", "inv", None),
        P("azim", "inv", None),
        P("azim", "inv"),
        P("inv", "azim", None),
    )
    return jax.shard_map(
        local,
        mesh=mesh,
        in_specs=placed,
        out_specs=(P("inv", "azim", None, None), P("azim", "inv", None)),
        check_vma=False,
    )
```
